32 devices in a mesh: grp: 2 (over x), seq: 16 (over z, y, core).
Axes of the slice: x: 2, y: 2, z: 4, core: 2. Of those that a mesh axis runs over, the one named last changes fastest.
Arguments:
- fast_state: bfloat16 [32, 3, 1024, 512], P(('grp', 'seq')), parts along dimension 0, may hold values from -0.25 to 0.25
- initial_fast: bfloat16 [3, 1024, 512], P(None, 'seq'), may hold values from -0.25 to 0.25
- queries: bfloat16 [32, 4, 384, 512], P(('grp', 'seq')), parts along dimension 0, may hold values from -6 to 6
- token_keys: bfloat16 [32, 4, 384, 512], P(('grp', 'seq')), parts along dimension 0, may hold values from -6 to 6
- token_values: bfloat16 [32, 4, 384, 512], P(('grp', 'seq')), parts along dimension 0, may hold values from -6 to 6
- step_sizes: bfloat16 [32, 4, 384], P(('grp', 'seq')), parts along dimension 0, may hold values from 0.0019989014 to 0.019897461
Outputs:
- layer_output: bfloat16 [32, 4, 384, 512], P(('grp', 'seq')), parts along dimension 0
The draws below stay inside these ranges and needn't reach their ends.
There are 2 independent parts, one for each index of `grp`. The reference program is written for one: setup_inputs(seed, part) draws one part's arguments, and reference() takes and returns one part's arrays. A program takes and returns all parts, laid end to end along the dimension named above; an argument that names none is the same for every part. Nothing has to cross between parts.
All inputs are finite; a program needn't handle non-finite values.
Results may differ from the reference program's by a relative error of at most 0.012.
The reference program's roundings to bfloat16 on the way count: a program that leaves them out, or rounds other values in their place, can miss the bound.
Values may be sent and summed in bfloat16 or wider, within the bound.
A program may use at most 64 MiB of HBM per device.

```python
import math
import jax
import jax.numpy as jnp
from jax import lax

DK = 512
HID = 1024
SPAN = 384
TICKS = 4
SECTIONS = 16


def shard_levels(own_key, extent, shards, least, high):
    factor_of = 1.0
    for position, blocks in shards:
        heights = jax.random.uniform(jax.random.fold_in(jax.random.fold_in(own_key, 6), position), (blocks,), jnp.float32, least / len(shards), high / len(shards))
        factor_of = factor_of * jnp.repeat(jnp.exp(heights), extent[position] // blocks).reshape((-1,) + (1,) * (len(extent) - 1 - position))
    return factor_of


def bell_draw(key, dims, width, most, cuts=(), dtype=jnp.bfloat16):
    array = jax.random.normal(key, dims, jnp.float32) * width
    if len(cuts) > 0:
        array = shard_levels(key, dims, cuts, -0.22, 0.18) * array
    return jnp.clip(array, min=-most, max=most).astype(dtype)


def setup_inputs(seed: int = 0, part: int = 0) -> dict:
    seeds = jax.random.split(jax.random.key(seed), 7)
    own_keys = jax.random.split(jax.random.fold_in(seeds[6], part), 7)
    return {
        "fast_state": bell_draw(own_keys[0], (SECTIONS, 3, HID, DK), DK ** -0.5, 0.25, ((0, 16),)),
        "initial_fast": bell_draw(seeds[1], (3, HID, DK), DK ** -0.5, 0.25, ((1, 16),)),
        "queries": bell_draw(own_keys[2], (SECTIONS, TICKS, SPAN, DK), 1.0, 6.0, ((0, 16),)),
        "token_keys": bell_draw(own_keys[3], (SECTIONS, TICKS, SPAN, DK), 1.0, 6.0, ((0, 16),)),
        "token_values": bell_draw(own_keys[4], (SECTIONS, TICKS, SPAN, DK), 1.0, 6.0, ((0, 16),)),
        "step_sizes": jnp.clip(jnp.exp(math.log(0.019897461) - 2.2979944 * jax.random.uniform(own_keys[5], (SECTIONS, TICKS, SPAN), jnp.float32) ** shard_levels(own_keys[5], (SECTIONS, TICKS, SPAN), ((0, 16),), -0.2, 0.2)), 0.0019989014, 0.019897461).astype(jnp.bfloat16),
    }


epsilon = 1e-06

def contract_last(left_side, right_side):
    return lax.dot_general(left_side, right_side, (((1,), (1,)), ((), ())), preferred_element_type=jnp.float32)

def contract_first(left_side, right_side):
    return lax.dot_general(left_side, right_side, (((0,), (0,)), ((), ())), preferred_element_type=jnp.float32)

def rescale(updated, previous):
    old_norm = jnp.sqrt(lax.optimization_barrier(jnp.sum(previous * previous, axis=-1, keepdims=True)) + epsilon)
    new_norm = jnp.sqrt(lax.optimization_barrier(jnp.sum(updated * updated, axis=-1, keepdims=True)) + epsilon)
    return updated * (old_norm / new_norm)

def advance(fast, token_keys, token_values, step_sizes):
    gate_pre = contract_last(token_keys, fast[0])
    up_pre = contract_last(token_keys, fast[1])
    gate_sig = jax.nn.sigmoid(gate_pre)
    hidden = (gate_pre * gate_sig * up_pre).astype(jnp.bfloat16)
    target = (step_sizes.astype(jnp.float32)[:, None] * token_values.astype(jnp.float32)).astype(jnp.bfloat16)
    back_grad = contract_last(target, fast[2])
    grad_gate = (back_grad * up_pre * gate_sig * (1.0 + gate_pre * (1.0 - gate_sig))).astype(jnp.bfloat16)
    grad_up = (back_grad * gate_pre * gate_sig).astype(jnp.bfloat16)
    delta_gate = contract_first(grad_gate, token_keys)
    delta_up = contract_first(grad_up, token_keys)
    delta_down = contract_first(hidden, target)
    previous = fast.astype(jnp.float32)
    updated = previous + jnp.stack([delta_gate, delta_up, delta_down])
    return rescale(updated, previous).astype(jnp.bfloat16)

def serve_queries(fast, queries):
    gate_pre = contract_last(queries, fast[0])
    up_pre = contract_last(queries, fast[1])
    hidden = (gate_pre * jax.nn.sigmoid(gate_pre) * up_pre).astype(jnp.bfloat16)
    return jnp.dot(hidden, fast[2], preferred_element_type=jnp.float32).astype(jnp.bfloat16)

def reference(fast_state, initial_fast, queries, token_keys, token_values, step_sizes):
    carried = fast_state
    results = []
    advanced = fast_state
    for step_index in range(TICKS):
        if step_index > 0:
            carried = jnp.concatenate([initial_fast[None], advanced[:-1]], axis=0)
        advanced = lax.map(lambda section_item: advance(*section_item), (carried, token_keys[:, step_index], token_values[:, step_index], step_sizes[:, step_index]))
        served = lax.map(lambda section_item: serve_queries(*section_item), (advanced, queries[:, step_index]))
        results.append(served)
    return jnp.stack(results, axis=1)
```

```python
import functools

import jax
import jax.numpy as jnp
from jax import lax
from jax.experimental import pallas as pl
from jax.experimental.pallas import tpu as pltpu
from jax.sharding import PartitionSpec as P

epsilon = 1e-06
AXIS = "seq"


def contract_last(left_side, right_side):
    return lax.dot_general(
        left_side, right_side, (((1,), (1,)), ((), ())), preferred_element_type=jnp.float32
    )


def plain_dot(left_side, right_side):
    return jnp.dot(left_side, right_side, preferred_element_type=jnp.float32)


def sigmoid(value):
    return 0.5 * jnp.tanh(0.5 * value) + 0.5


def rescale(updated, previous):
    old_square = jnp.sum(previous * previous, axis=-1, keepdims=True) + epsilon
    new_square = jnp.sum(updated * updated, axis=-1, keepdims=True) + epsilon
    return (updated * (jnp.sqrt(old_square) * lax.rsqrt(new_square))).astype(jnp.bfloat16)


def kernel(
    n, ticks, part,
    fast, init, k_in, t_in, q_in, out,
    st, ini, kb, tb, qb, ans, acc,
    local_sem, own_sem, data_send, data_recv, ans_send, ans_recv, init_send, init_recv, fwd_send, fwd_recv,
):
    p = lax.axis_index(AXIS)
    last = n - 1
    reach = ticks - 1
    hid = st.shape[1]

    def local_copies():
        return [
            pltpu.make_async_copy(k_in.at[0, 0], kb.at[0], local_sem.at[0]),
            pltpu.make_async_copy(t_in.at[0], tb.at[0], local_sem.at[1]),
            pltpu.make_async_copy(fast.at[0], st, local_sem.at[2]),
            pltpu.make_async_copy(q_in.at[0, 0], qb.at[0], local_sem.at[3]),
        ]

    def data_copies(t):
        dest = lax.rem(p - t + n, n)
        pairs = [(k_in.at[0, t], kb.at[t]), (t_in.at[t], tb.at[t]), (q_in.at[0, t], qb.at[t])]
        return [
            pltpu.make_async_remote_copy(
                src_ref=src, dst_ref=dst,
                send_sem=data_send.at[t, i], recv_sem=data_recv.at[t, i],
                device_id={AXIS: dest}, device_id_type=pl.DeviceIdType.MESH,
            )
            for i, (src, dst) in enumerate(pairs)
        ]

    def answer_copy(t):
        return pltpu.make_async_remote_copy(
            src_ref=ans.at[t], dst_ref=out.at[0, t],
            send_sem=ans_send.at[t], recv_sem=ans_recv.at[t],
            device_id={AXIS: lax.rem(p + t, n)}, device_id_type=pl.DeviceIdType.MESH,
        )

    def shard_copy(i):
        return pltpu.make_async_remote_copy(
            src_ref=init, dst_ref=ini.at[i],
            send_sem=init_send, recv_sem=init_recv.at[i],
            device_id={AXIS: last}, device_id_type=pl.DeviceIdType.MESH,
        )

    def forward_copy(i):
        return pltpu.make_async_remote_copy(
            src_ref=ini, dst_ref=ini,
            send_sem=fwd_send.at[i], recv_sem=fwd_recv,
            device_id={AXIS: last - i}, device_id_type=pl.DeviceIdType.MESH,
        )

    own_shard = pltpu.make_async_copy(init, ini.at[last], own_sem)

    for copy in local_copies():
        copy.start()

    barrier = pltpu.get_barrier_semaphore()
    for off in range(1, ticks):
        for other in (lax.rem(p + off, n), lax.rem(p - off + n, n)):
            pl.semaphore_signal(
                barrier, inc=1, device_id={AXIS: other}, device_id_type=pl.DeviceIdType.MESH
            )
    far_from, far_to = reach, n - 1 - reach
    far = jnp.logical_and(p >= far_from, p < far_to)

    @pl.when(far)
    def _():
        pl.semaphore_signal(
            barrier, inc=1, device_id={AXIS: last}, device_id_type=pl.DeviceIdType.MESH
        )
        pl.semaphore_wait(barrier, 2 * reach + 1)

    @pl.when(p == last)
    def _():
        @pl.loop(far_from, far_to)
        def _(i):
            pl.semaphore_signal(
                barrier, inc=1, device_id={AXIS: i}, device_id_type=pl.DeviceIdType.MESH
            )

        pl.semaphore_wait(barrier, 2 * reach + (far_to - far_from))

    @pl.when(jnp.logical_and(jnp.logical_not(far), p != last))
    def _():
        pl.semaphore_wait(barrier, 2 * reach)

    for t in range(1, ticks):
        for copy in data_copies(t):
            copy.start()
        if t == 1:
            @pl.when(p == last)
            def _():
                own_shard.start()

            @pl.when(p != last)
            def _():
                shard_copy(p).start()

    for copy in local_copies():
        copy.wait()

    @pl.loop(0, ticks)
    def _(t):
        @pl.when(t > 0)
        def _():
            for copy in data_copies(t):
                copy.wait_recv()

        @pl.when(jnp.logical_and(t > 0, p + t == n))
        def _():
            @pl.when(p == last)
            def _():
                own_shard.wait()

                @pl.loop(0, last)
                def _(i):
                    shard_copy(i).wait_recv()

                for i in range(1, reach):
                    forward_copy(i).start()

            @pl.when(p != last)
            def _():
                forward_copy(1).wait_recv()

            rows = init.shape[1]
            for i in range(n):
                for m in range(3):
                    st[m, pl.ds(i * rows, rows), :] = ini[i, m]

        @pl.loop(0, hid // part)
        def _(c):
            span = pl.ds(pl.multiple_of(c * part, part), part)
            keys, target, asked = kb[t], tb[t], qb[t]
            gate, up, down = st[0, span, :], st[1, span, :], st[2, span, :]
            gate_pre = contract_last(gate, keys)
            up_pre = contract_last(up, keys)
            back_grad = contract_last(down, target)
            sig = sigmoid(gate_pre)
            silu = gate_pre * sig
            hidden = (silu * up_pre).astype(jnp.bfloat16)
            grad_gate = (
                back_grad * up_pre * sig * (1.0 + gate_pre * (1.0 - sig))
            ).astype(jnp.bfloat16)
            grad_up = (back_grad * silu).astype(jnp.bfloat16)
            old_gate = gate.astype(jnp.float32)
            old_up = up.astype(jnp.float32)
            old_down = down.astype(jnp.float32)
            new_gate = rescale(old_gate + plain_dot(grad_gate, keys), old_gate)
            new_up = rescale(old_up + plain_dot(grad_up, keys), old_up)
            new_down = rescale(old_down + plain_dot(hidden, target), old_down)
            st[0, span, :] = new_gate
            st[1, span, :] = new_up
            st[2, span, :] = new_down
            pre = contract_last(asked, new_gate)
            ahead = contract_last(asked, new_up)
            served = (pre * sigmoid(pre) * ahead).astype(jnp.bfloat16)
            term = plain_dot(served, new_down)

            @pl.when(c == 0)
            def _():
                acc[...] = term

            @pl.when(c > 0)
            def _():
                acc[...] += term

        ans[t] = acc[...].astype(jnp.bfloat16)

        @pl.when(t == 0)
        def _():
            pltpu.make_async_copy(ans.at[0], out.at[0, 0], local_sem.at[0]).start()

        @pl.when(t > 0)
        def _():
            answer_copy(t).start()

    pltpu.make_async_copy(ans.at[0], out.at[0, 0], local_sem.at[0]).wait()
    for t in range(1, ticks):
        for copy in data_copies(t):
            copy.wait_send()
        answer_copy(t).wait_send()
        answer_copy(t).wait_recv()

    @pl.when(p == last)
    def _():
        for i in range(1, reach):
            forward_copy(i).wait_send()

    @pl.when(p != last)
    def _():
        shard_copy(p).wait_send()


def body(fast_state, initial_fast, queries, token_keys, token_values, step_sizes):
    n = lax.axis_size(AXIS)
    _, ticks, span, width = queries.shape
    hid = fast_state.shape[2]
    target = (
        step_sizes[0].astype(jnp.float32)[:, :, None] * token_values[0].astype(jnp.float32)
    ).astype(jnp.bfloat16)
    slots = pltpu.VMEM((ticks, span, width), jnp.bfloat16)
    dma = pltpu.SemaphoreType.DMA
    anywhere = pl.BlockSpec(memory_space=pl.ANY)
    return pl.pallas_call(
        functools.partial(kernel, n, ticks, 256),
        out_shape=jax.ShapeDtypeStruct(queries.shape, jnp.bfloat16),
        in_specs=[anywhere] * 5,
        out_specs=anywhere,
        scratch_shapes=[
            pltpu.VMEM(fast_state.shape[1:], jnp.bfloat16),
            pltpu.VMEM((n,) + initial_fast.shape, jnp.bfloat16),
            slots, slots, slots, slots,
            pltpu.VMEM((span, width), jnp.float32),
            dma((4,)), dma, dma((ticks, 3)), dma((ticks, 3)), dma((ticks,)), dma((ticks,)),
            dma, dma((n,)), dma((ticks,)), dma,
        ],
        compiler_params=pltpu.CompilerParams(
            collective_id=0, has_side_effects=True, vmem_limit_bytes=48 * 1024 * 1024
        ),
        cost_estimate=pl.CostEstimate(
            flops=18 * ticks * span * width * hid,
            bytes_accessed=16 * 1024 * 1024,
            transcendentals=2 * ticks * span * hid,
        ),
    )(fast_state, initial_fast, token_keys, target, queries)


def solution(mesh):
    return jax.shard_map(
        body,
        mesh=mesh,
        in_specs=(
            P(("grp", AXIS), None, None, None),
            P(None, AXIS, None),
            P(("grp", AXIS), None, None, None),
            P(("grp", AXIS), None, None, None),
            P(("grp", AXIS), None, None, None),
            P(("grp", AXIS), None, None),
        ),
        out_specs=P(("grp", AXIS), None, None, None),
        check_vma=False,
    )
```

```python
import functools

import jax
import jax.numpy as jnp
from jax import lax
from jax.experimental import pallas as pl
from jax.experimental.pallas import tpu as pltpu
from jax.sharding import PartitionSpec as P

epsilon = 1e-06
AXIS = "seq"


def contract_last(left_side, right_side):
    return lax.dot_general(
        left_side, right_side, (((1,), (1,)), ((), ())), preferred_element_type=jnp.float32
    )


def plain_dot(left_side, right_side):
    return jnp.dot(left_side, right_side, preferred_element_type=jnp.float32)


def sigmoid(value):
    return 0.5 * jnp.tanh(0.5 * value) + 0.5


def rescale(updated, previous):
    old_square = jnp.sum(previous * previous, axis=-1, keepdims=True) + epsilon
    new_square = jnp.sum(updated * updated, axis=-1, keepdims=True) + epsilon
    return (updated * (jnp.sqrt(old_square) * lax.rsqrt(new_square))).astype(jnp.bfloat16)


def restarts(ticks):
    units = []
    filled = [ticks - 1, ticks - 1]
    for late in range(1, ticks):
        device = 0 if late == 1 else 1
        for tick in range(late, ticks):
            units.append((device, filled[device], tick - late, tick, tick == late))
            filled[device] += 1
    return units, max(filled)


def kernel(
    n, ticks, part,
    fast, init, k_in, t_in, q_in, out,
    st, ini, kb, tb, qb, ans, acc,
    local_sem, own_sem, data_send, data_recv, ans_send, ans_recv, init_send, init_recv, fwd_send, fwd_recv,
):
    p = lax.axis_index(AXIS)
    reach = ticks - 1
    hid = st.shape[2]
    extra, final = restarts(ticks)
    slot_of = list(range(reach)) + [final]

    def local_copies():
        return [
            pltpu.make_async_copy(k_in.at[0, 0], kb.at[0], local_sem.at[0]),
            pltpu.make_async_copy(t_in.at[0], tb.at[0], local_sem.at[1]),
            pltpu.make_async_copy(fast.at[0], st.at[0], local_sem.at[2]),
            pltpu.make_async_copy(q_in.at[0, 0], qb.at[0], local_sem.at[3]),
        ]

    def pairs(t, slot):
        return [
            (k_in.at[0, t], kb.at[slot]), (t_in.at[t], tb.at[slot]), (q_in.at[0, t], qb.at[slot])
        ]

    def remote(src, dst, send, recv, dest):
        return pltpu.make_async_remote_copy(
            src_ref=src, dst_ref=dst, send_sem=send, recv_sem=recv,
            device_id={AXIS: dest}, device_id_type=pl.DeviceIdType.MESH,
        )

    def data_copies(t, slot, dest):
        return [
            remote(src, dst, data_send.at[t, i], data_recv.at[slot, i], dest)
            for i, (src, dst) in enumerate(pairs(t, slot))
        ]

    def own_copies(t, slot):
        return [
            pltpu.make_async_copy(src, dst, data_recv.at[slot, i])
            for i, (src, dst) in enumerate(pairs(t, slot))
        ]

    def answer_copy(slot, t, home):
        return remote(ans.at[slot], out.at[0, t], ans_send.at[slot], ans_recv.at[t], home)

    def own_answer(slot, t):
        return pltpu.make_async_copy(ans.at[slot], out.at[0, t], ans_recv.at[t])

    def shard_copy(i):
        return remote(init, ini.at[i], init_send, init_recv.at[i], 0)

    def forward_copy():
        return remote(ini, ini, fwd_send, fwd_recv, 1)

    def signal(other):
        pl.semaphore_signal(
            barrier, inc=1, device_id={AXIS: other}, device_id_type=pl.DeviceIdType.MESH
        )

    own_shard = pltpu.make_async_copy(init, ini.at[0], own_sem)

    for copy in local_copies():
        copy.start()

    barrier = pltpu.get_barrier_semaphore()
    for off in range(1, ticks):
        @pl.when(p + off < n)
        def _():
            signal(p + off)

        @pl.when(p >= off)
        def _():
            signal(p - off)

    @pl.when(p > reach)
    def _():
        signal(0)

    @pl.when(p == 0)
    def _():
        @pl.loop(ticks, n)
        def _(i):
            signal(i)

        pl.semaphore_wait(barrier, n - 1)

    for off in range(1, ticks):
        @pl.when(p == off)
        def _():
            pl.semaphore_wait(barrier, off + min(reach, n - 1 - off))

        @pl.when(p == n - off)
        def _():
            pl.semaphore_wait(barrier, reach + off)

    @pl.when(jnp.logical_and(p > reach, p < n - reach))
    def _():
        pl.semaphore_wait(barrier, 2 * reach + 1)

    @pl.when(p == 0)
    def _():
        own_shard.start()

    @pl.when(p > 0)
    def _():
        shard_copy(p).start()

    for t in range(1, ticks):
        @pl.when(p >= t)
        def _():
            for copy in data_copies(t, slot_of[t], p - t):
                copy.start()

        for device, slot, section, tick, _fresh in extra:
            if tick == t:
                @pl.when(p == section)
                def _():
                    moves = (
                        own_copies(t, slot) if device == section else data_copies(t, slot, device)
                    )
                    for copy in moves:
                        copy.start()


    for copy in local_copies():
        copy.wait()

    def unpack():
        rows = init.shape[1]
        for i in range(n):
            for m in range(3):
                st[1, m, pl.ds(i * rows, rows), :] = ini[i, m]

    def run(step):
        which = lax.rem(step // reach, 2)

        @pl.when(step > 0)
        def _():
            for copy in own_copies(1, step):
                copy.wait()

        @pl.when(jnp.logical_and(step == reach, p == 0))
        def _():
            own_shard.wait()

            @pl.loop(1, n)
            def _(i):
                shard_copy(i).wait_recv()

            forward_copy().start()

        @pl.when(jnp.logical_and(step == reach, p == 1))
        def _():
            forward_copy().wait_recv()

        for device, slot, _section, _tick, fresh in extra:
            if fresh:
                @pl.when(jnp.logical_and(step == slot, p == device))
                def _():
                    unpack()

        @pl.loop(0, hid // part, unroll=True)
        def _(c):
            span = pl.ds(pl.multiple_of(c * part, part), part)
            keys, target, asked = kb[step], tb[step], qb[step]
            gate, up, down = st[which, 0, span, :], st[which, 1, span, :], st[which, 2, span, :]
            gate_pre = contract_last(gate, keys)
            up_pre = contract_last(up, keys)
            back_grad = contract_last(down, target)
            sig = sigmoid(gate_pre)
            silu = gate_pre * sig
            hidden = (silu * up_pre).astype(jnp.bfloat16)
            grad_gate = (
                back_grad * up_pre * sig * (1.0 + gate_pre * (1.0 - sig))
            ).astype(jnp.bfloat16)
            grad_up = (back_grad * silu).astype(jnp.bfloat16)
            old_gate = gate.astype(jnp.float32)
            old_up = up.astype(jnp.float32)
            old_down = down.astype(jnp.float32)
            new_gate = rescale(old_gate + plain_dot(grad_gate, keys), old_gate)
            new_up = rescale(old_up + plain_dot(grad_up, keys), old_up)
            new_down = rescale(old_down + plain_dot(hidden, target), old_down)
            st[which, 0, span, :] = new_gate
            st[which, 1, span, :] = new_up
            st[which, 2, span, :] = new_down
            pre = contract_last(asked, new_gate)
            ahead = contract_last(asked, new_up)
            served = (pre * sigmoid(pre) * ahead).astype(jnp.bfloat16)
            term = plain_dot(served, new_down)

            @pl.when(c == 0)
            def _():
                acc[...] = term

            @pl.when(c > 0)
            def _():
                acc[...] += term

        ans[step] = acc[...].astype(jnp.bfloat16)

        @pl.when(step == 0)
        def _():
            own_answer(0, 0).start()

        for t in range(1, ticks):
            @pl.when(step == slot_of[t])
            def _():
                answer_copy(slot_of[t], t, p + t).start()

        for device, slot, section, tick, _fresh in extra:
            @pl.when(jnp.logical_and(step == slot, p == device))
            def _():
                if device == section:
                    own_answer(slot, tick).start()
                else:
                    answer_copy(slot, tick, section).start()

    @pl.loop(0, final + 1)
    def _(step):
        middle = jnp.logical_and(step >= reach, step < final)
        tick = step - (step // final) * (final - reach)
        chain = jnp.logical_and(jnp.logical_not(middle), p + tick < n)

        @pl.when(jnp.logical_or(chain, jnp.logical_and(middle, p < 2)))
        def _():
            run(step)

    for t in range(ticks):
        own_answer(0, t).wait()
    for t in range(1, ticks):
        @pl.when(p >= t)
        def _():
            for copy in data_copies(t, slot_of[t], p - t):
                copy.wait_send()

        @pl.when(p + t < n)
        def _():
            answer_copy(slot_of[t], t, p + t).wait_send()

    for device, slot, section, tick, _fresh in extra:
        if device != section:
            @pl.when(p == section)
            def _():
                for copy in data_copies(tick, slot, device):
                    copy.wait_send()

            @pl.when(p == device)
            def _():
                answer_copy(slot, tick, section).wait_send()

    @pl.when(p == 0)
    def _():
        forward_copy().wait_send()

    @pl.when(p > 0)
    def _():
        shard_copy(p).wait_send()


def body(fast_state, initial_fast, queries, token_keys, token_values, step_sizes):
    n = lax.axis_size(AXIS)
    _, ticks, span, width = queries.shape
    hid = fast_state.shape[2]
    target = (
        step_sizes[0].astype(jnp.float32)[:, :, None] * token_values[0].astype(jnp.float32)
    ).astype(jnp.bfloat16)
    held = restarts(ticks)[1] + 1
    slots = pltpu.VMEM((held, span, width), jnp.bfloat16)
    dma = pltpu.SemaphoreType.DMA
    anywhere = pl.BlockSpec(memory_space=pl.ANY)
    return pl.pallas_call(
        functools.partial(kernel, n, ticks, 256),
        out_shape=jax.ShapeDtypeStruct(queries.shape, jnp.bfloat16),
        in_specs=[anywhere] * 5,
        out_specs=anywhere,
        scratch_shapes=[
            pltpu.VMEM((2,) + fast_state.shape[1:], jnp.bfloat16),
            pltpu.VMEM((n,) + initial_fast.shape, jnp.bfloat16),
            slots, slots, slots, slots,
            pltpu.VMEM((span, width), jnp.float32),
            dma((4,)), dma, dma((ticks, 3)), dma((held, 3)), dma((held,)), dma((ticks,)),
            dma, dma((n,)), dma, dma,
        ],
        compiler_params=pltpu.CompilerParams(
            collective_id=0, has_side_effects=True, vmem_limit_bytes=48 * 1024 * 1024
        ),
        cost_estimate=pl.CostEstimate(
            flops=18 * ticks * span * width * hid,
            bytes_accessed=16 * 1024 * 1024,
            transcendentals=2 * ticks * span * hid,
        ),
    )(fast_state, initial_fast, token_keys, target, queries)


def solution(mesh):
    return jax.shard_map(
        body,
        mesh=mesh,
        in_specs=(
            P(("grp", AXIS), None, None, None),
            P(None, AXIS, None),
            P(("grp", AXIS), None, None, None),
            P(("grp", AXIS), None, None, None),
            P(("grp", AXIS), None, None, None),
            P(("grp", AXIS), None, None),
        ),
        out_specs=P(("grp", AXIS), None, None, None),
        check_vma=False,
    )
```
